32 devices in a mesh: basin: 8 (over z, x), ens: 4 (over y, core).
Axes of the slice: x: 2, y: 2, z: 4, core: 2. Of those that a mesh axis runs over, the one named last changes fastest.
Arguments:
- downstream: int32 [8192], P('basin'), may hold values from 0 to 8191, as said below
- bed_level: float32 [8192], P('basin'), may hold values from 0 to 3
- reach_length: float32 [8192], P('basin'), may hold values from 1000 to 5000
- channel_width: float32 [8192], P('basin'), may hold values from 50 to 300
- roughness: float32 [8192], P('basin'), may hold values from 0.025 to 0.06
- depth: float32 [8192, 512], P('basin', 'ens'), may hold values from 0.5 to 3
- flow: float32 [8192, 512], P('basin', 'ens'), may hold values from 0 to 2
- runoff: float32 [8192, 512], P('basin', 'ens'), may hold values from 0.0002 to 0.005
Outputs:
- new_depth: float32 [8192, 512], P('basin', 'ens')
- new_flow: float32 [8192, 512], P('basin', 'ens')
- mean_flow: float32 [8192], P('basin')
The draws below stay inside these ranges and needn't reach their ends.
Inputs may be any that keep to these rules, and one draw needn't show every extreme that they name: `downstream`: within the 1024 cells of one block, a cell drains either into a later cell of the same block, into itself (mouth), or into a cell of the next block or of the block after it along basin (main-stem segments); from one block at most 256 cells drain into each of these two, and exactly 256 into the next one wherever it exists.
All inputs are finite; a program needn't handle non-finite values.
Results may differ from the reference program's by a relative error of at most 0.0001.
Values sent between devices are 32-bit elements; how exact they have to be, the bound alone decides.
A program may use at most 64 MiB of HBM per device.

```python
import math
import jax
import jax.numpy as jnp

CELL_DEV = 1024
ENS = 512
SLOTS = 256
STEPS = 4
CELLS = 8192
N_BASIN = 8


def draw_downstream(key, part):
    count = CELL_DEV
    inner = count - 2 * SLOTS
    device = jnp.arange(N_BASIN, dtype=jnp.int32)[:, None]
    place = jnp.arange(count, dtype=jnp.int32)[None, :]
    first_key = jax.random.fold_in(key, 11)
    second_key = jax.random.fold_in(key, 12)
    third_key = jax.random.fold_in(key, 13)
    order_key = jax.random.fold_in(key, 14)
    block_keys = jax.random.split(order_key, N_BASIN)
    rank = jax.vmap(lambda one: jax.random.permutation(one, count))(block_keys).astype(jnp.int32)
    spread_bits = jax.random.randint(first_key, (N_BASIN, count), 0, 2 ** 30)
    room = jnp.maximum(count - 1 - place, 1)
    local_down = place + 1 + spread_bits % room
    local_down = jnp.where(place == count - 1, place, local_down)
    group = (rank - inner) // SLOTS
    target_device = device + 1 + group
    target_cell = jax.random.randint(second_key, (N_BASIN, count), 0, count)
    live = (jax.random.randint(third_key, (N_BASIN, count), 0, 10) < 7) | (group == 0)
    live = live & (target_device < N_BASIN)
    remote_down = jnp.where(live, target_device * count + target_cell, device * count + place)
    result = jnp.where(rank < inner, device * count + local_down, remote_down)
    return result.reshape(-1).astype(jnp.int32)


def level_of(rng, dims, pieces, low, top_value):
    def one(axis_at, blocks):
        heights = jax.random.uniform(jax.random.fold_in(jax.random.fold_in(rng, 6), axis_at), (blocks,), jnp.float32, low / len(pieces), top_value / len(pieces))
        return jnp.repeat(jnp.exp(heights), dims[axis_at] // blocks).reshape((-1,) + (1,) * (len(dims) - axis_at - 1))

    factor_of = one(*pieces[0])
    for cut in pieces[1:]:
        factor_of = factor_of * one(*cut)
    return factor_of


def setup_inputs(seed: int = 0) -> dict:
    arg_keys = jax.random.split(jax.random.key(seed), 9)
    downstream = draw_downstream(jax.random.fold_in(arg_keys[8], 71), 0)
    bed_level = jnp.clip(3.0 * jax.random.uniform(arg_keys[1], (CELLS,), jnp.float32) ** level_of(arg_keys[1], (CELLS,), ((0, 8),), -0.2, 0.2), 0.0, 3.0)
    reach_length = jnp.clip(jnp.exp(math.log(5000.0) - 1.609438 * jax.random.uniform(arg_keys[2], (CELLS,), jnp.float32) ** level_of(arg_keys[2], (CELLS,), ((0, 8),), -0.2, 0.2)), 1000.0, 5000.0)
    channel_width = jnp.clip(jnp.exp(math.log(300.0) - 1.7917595 * jax.random.uniform(arg_keys[3], (CELLS,), jnp.float32) ** level_of(arg_keys[3], (CELLS,), ((0, 8),), -0.2, 0.2)), 50.0, 300.0)
    roughness = jnp.clip(jnp.exp(math.log(0.06) - 0.8754687 * jax.random.uniform(arg_keys[4], (CELLS,), jnp.float32) ** level_of(arg_keys[4], (CELLS,), ((0, 8),), -0.2, 0.2)), 0.025, 0.06)
    depth = jnp.clip(0.5 + 2.5 * jax.random.uniform(arg_keys[5], (CELLS, ENS), jnp.float32) ** level_of(arg_keys[5], (CELLS, ENS), ((0, 8), (1, 4)), -0.2, 0.2), 0.5, 3.0)
    flow = jnp.clip(2.0 * jax.random.uniform(arg_keys[6], (CELLS, ENS), jnp.float32) ** level_of(arg_keys[6], (CELLS, ENS), ((0, 8), (1, 4)), -0.2, 0.2), 0.0, 2.0)
    runoff = jnp.clip(jnp.exp(math.log(0.005) - 3.218876 * jax.random.uniform(arg_keys[7], (CELLS, ENS), jnp.float32) ** level_of(arg_keys[7], (CELLS, ENS), ((0, 8), (1, 4)), -0.2, 0.2)), 0.0002, 0.005)
    return dict(downstream=downstream, bed_level=bed_level, reach_length=reach_length, channel_width=channel_width, roughness=roughness, depth=depth, flow=flow, runoff=runoff)


GRAVITY = 9.81
TIME_STEP = 30.0
DEPTH_FLOOR = 0.25


def momentum(flow, depth, bed, level_down, bed_down, length, rough):
    level = bed + depth
    flow_depth = jnp.maximum(jnp.maximum(level, level_down) - jnp.maximum(bed, bed_down), DEPTH_FLOOR)
    slope = (level_down - level) / length
    friction = 1.0 + GRAVITY * TIME_STEP * rough * rough * jnp.abs(flow) / flow_depth ** (7.0 / 3.0)
    moved = (flow - GRAVITY * TIME_STEP * flow_depth * slope) / friction
    return jnp.minimum(moved, depth * length / (2.0 * TIME_STEP))


def reference(downstream, bed_level, reach_length, channel_width, roughness, depth, flow, runoff):
    count = downstream.shape[0]
    own = jnp.arange(count, dtype=jnp.int32)
    mouth = downstream == own
    bed_down = jnp.where(mouth, bed_level - 1.0, bed_level[downstream])
    area = (channel_width * reach_length)[:, None]
    for step in range(STEPS):
        level = bed_level[:, None] + depth
        level_down = jnp.where(mouth[:, None], bed_down[:, None], level[downstream])
        flow = momentum(flow, depth, bed_level[:, None], level_down, bed_down[:, None], reach_length[:, None], roughness[:, None])
        discharge = flow * channel_width[:, None]
        arriving = jax.ops.segment_sum(jnp.where(mouth[:, None], jnp.zeros_like(discharge), discharge), downstream, num_segments=count)
        depth = depth + TIME_STEP * (runoff + (arriving - discharge) / area)
    return depth, flow, jnp.sum(flow, axis=1) / ENS
```

```python
import functools

import jax
import jax.numpy as jnp
from jax import lax
from jax.experimental import pallas as pl
from jax.experimental.pallas import tpu as pltpu
from jax.sharding import PartitionSpec as P

SLOTS = 256
STEPS = 4
GRAVITY = 9.81
TIME_STEP = 30.0
DEPTH_FLOOR = 0.25

BF16 = jnp.bfloat16
F32 = jnp.float32
MESH = pl.DeviceIdType.MESH

T_LOCAL, T_REMOTE, BED, BED_DOWN, SLOPE_K, CAP, WIDTH, FRICTION, INV_AREA = range(9)
M_HEAD, M_TABLE, M_FLOW, M_DOWN, M_UP = 0, 2, 4, 6, 6 + 2 * STEPS
M_SUM = 6 + 4 * STEPS


def dot(a, b):
    return jnp.dot(a, b, preferred_element_type=F32)


def dot_nt(a, b):
    return lax.dot_general(a, b, (((1,), (1,)), ((), ())), preferred_element_type=F32)


def pieces(x):
    high = x.astype(BF16)
    rest = x - high.astype(F32)
    middle = rest.astype(BF16)
    low = (rest - middle.astype(F32)).astype(BF16)
    return jnp.concatenate([high, middle, low], axis=0)


def halves(x):
    high = x.astype(BF16)
    return high, (x - high.astype(F32)).astype(BF16)


def kernel(
    n_basin, n_ens, ds_ref, bed_ref, len_ref, wid_ref, rough_ref, depth_ref, flow_ref, runoff_ref,
    new_depth, new_flow, mean_out,
    head, head_in, table, table_in, perm, unperm, tmap, emap, smap, par, h_buf, q_buf, r_buf,
    split_a, split_b, split_c, hd_buf, up_out, up_in, down_in, acc, edge_split, sums, sums_in,
    send_sem, recv_sem,
):
    count = depth_ref.shape[0]
    members = depth_ref.shape[1]
    tiles = count // 128
    p = lax.axis_index("basin")
    e = lax.axis_index("ens")

    def dn(index, hop, src, dst):
        return pltpu.make_async_remote_copy(
            src_ref=src, dst_ref=dst, send_sem=send_sem.at[index + hop],
            recv_sem=recv_sem.at[index + hop],
            device_id={"basin": lax.rem(p + hop + 1, n_basin)}, device_id_type=MESH,
        )

    def up(index, hop, src, dst):
        return pltpu.make_async_remote_copy(
            src_ref=src, dst_ref=dst, send_sem=send_sem.at[index + hop],
            recv_sem=recv_sem.at[index + hop],
            device_id={"basin": lax.rem(p + n_basin - hop - 1, n_basin)}, device_id_type=MESH,
        )

    def has_lower(hop):
        return p + (hop + 1) < n_basin

    def has_upper(hop):
        return p >= hop + 1

    barrier = pltpu.get_barrier_semaphore()
    for hop in range(2):
        @pl.when(has_lower(hop))
        def _(hop=hop):
            pl.semaphore_signal(barrier, inc=1, device_id={"basin": p + hop + 1}, device_id_type=MESH)

        @pl.when(has_upper(hop))
        def _(hop=hop):
            pl.semaphore_signal(barrier, inc=1, device_id={"basin": p - hop - 1}, device_id_type=MESH)
    for d in range(1, n_ens):
        pl.semaphore_signal(barrier, inc=1, device_id={"ens": lax.rem(e + d, n_ens)}, device_id_type=MESH)

    rel = ds_ref[...] - p * count
    own = lax.broadcasted_iota(jnp.int32, (tiles, 128), 0) * 128 + lax.broadcasted_iota(
        jnp.int32, (tiles, 128), 1
    )
    near = (rel >= count) & (rel < 2 * count)
    far = rel >= 2 * count
    mouth = rel == own
    target = rel - jnp.where(near, count, 0) - jnp.where(far, 2 * count, 0)
    kind = jnp.where(near, 1.0, jnp.where(far, 2.0, jnp.where(mouth, 3.0, 0.0)))
    before = (
        lax.broadcasted_iota(jnp.int32, (128, 128), 0) < lax.broadcasted_iota(jnp.int32, (128, 128), 1)
    ).astype(BF16)
    ones = jnp.ones((128, 128), BF16)

    def ranks(mask):
        m = mask.astype(F32).astype(BF16)
        within = dot(m, before)
        totals = dot(m, ones)
        offsets, total = [], jnp.zeros((1, 128), F32)
        for t in range(tiles):
            offsets.append(total)
            total = total + totals[t:t + 1]
        return within + jnp.concatenate(offsets, axis=0), total

    rank1, n1 = ranks(near)
    rank2, n2 = ranks(far)
    rank0, _ = ranks(jnp.logical_not(near | far))
    gap1 = SLOTS - n1
    gap2 = SLOTS - n2
    place0 = jnp.where(
        rank0 < gap1, n1 + rank0,
        jnp.where(rank0 < gap1 + gap2, SLOTS + n2 + (rank0 - gap1), n1 + n2 + rank0),
    )
    place = jnp.where(near, rank1, jnp.where(far, SLOTS + rank2, place0))

    def to_row(ref, row, value):
        for t in range(tiles):
            ref[row:row + 1, t * 128:(t + 1) * 128] = value[t:t + 1]

    length = len_ref[...]
    width = wid_ref[...]
    rough = rough_ref[...]
    to_row(head, 0, place)
    to_row(head, 1, bed_ref[...])
    to_row(head, 2, target.astype(F32))
    to_row(head, 3, kind)
    head[4:8] = jnp.zeros((4, count), F32)
    to_row(table, SLOPE_K, (GRAVITY * TIME_STEP) / length)
    to_row(table, CAP, length / (2.0 * TIME_STEP))
    to_row(table, WIDTH, width)
    to_row(table, FRICTION, GRAVITY * TIME_STEP * rough * rough)
    to_row(table, INV_AREA, TIME_STEP / (width * length))

    peers = n_ens - 1
    for hop in range(2):
        peers = peers + lax.div(p + (n_basin - hop - 1), n_basin)
        peers = peers + lax.div(2 * n_basin - p - hop - 2, n_basin)
    pl.semaphore_wait(barrier, peers)

    for hop in range(2):
        @pl.when(has_upper(hop))
        def _(hop=hop):
            up(M_HEAD, hop, head, head_in.at[hop]).start()

    for hop in range(2):
        @pl.when(jnp.logical_not(has_upper(hop)))
        def _(hop=hop):
            rows = lax.broadcasted_iota(jnp.int32, (8, SLOTS), 0)
            table_in[hop] = jnp.where(rows == T_REMOTE, -1.0, 1.0)
            q_buf[count + hop * SLOTS:count + (hop + 1) * SLOTS] = jnp.zeros((SLOTS, members), F32)
            for step in range(STEPS):
                down_in[step, hop] = jnp.zeros((SLOTS, members), F32)

        @pl.when(jnp.logical_not(has_lower(hop)))
        def _(hop=hop):
            head_in[hop] = jnp.zeros((8, count), F32)
            for step in range(STEPS):
                up_in[step, hop] = jnp.zeros((SLOTS, members), F32)

    def one_hot_rows(ref, index_row, base, columns):
        def body(t, carry):
            rows = pl.ds(pl.multiple_of(t * 64, 64), 64)
            at = (lax.broadcasted_iota(jnp.int32, (64, columns), 0) + t * 64).astype(F32)
            ref[rows, base:base + columns] = jnp.where(at == index_row, 1.0, 0.0).astype(BF16)
            return carry
        lax.fori_loop(0, count // 64, body, 0)

    one_hot_rows(perm, head[0:1, :], 0, count)

    def split_into(dst, src):
        def body(t, carry):
            rows = pl.ds(pl.multiple_of(t * 128, 128), 128)
            high, low = halves(src[rows, :])
            dst[rows, :members] = high
            dst[rows, members:] = low
            return carry
        lax.fori_loop(0, count // 128, body, 0)

    split_into(split_a, depth_ref)
    split_into(split_b, flow_ref)
    split_into(split_c, runoff_ref)

    def joined(a, b):
        out = dot(a, b)
        return out[:, :members] + out[:, members:]

    def chunk(c, size=SLOTS):
        return slice(c * size, (c + 1) * size)

    for c in range(count // SLOTS):
        h_buf[0, chunk(c)] = joined(perm[chunk(c)], split_a[...])
        q_buf[chunk(c)] = joined(perm[chunk(c)], split_b[...])
        if c < 2:
            @pl.when(has_lower(c))
            def _(c=c):
                dn(M_FLOW, c, q_buf.at[pl.ds(c * SLOTS, SLOTS)], q_buf.at[pl.ds(count + c * SLOTS, SLOTS)]).start()
                dn(M_DOWN, c, h_buf.at[0, pl.ds(c * SLOTS, SLOTS)], down_in.at[0, c]).start()

    one_hot_rows(tmap, head[2:3, :], 0, count)
    for hop in range(2):
        @pl.when(has_lower(hop))
        def _(hop=hop):
            up(M_HEAD, hop, head, head_in.at[hop]).wait_recv()
    looked = jnp.concatenate([head[...], head_in[0], head_in[1], jnp.zeros((8, count), F32)], axis=0)
    found3 = dot(pieces(looked), tmap[...])
    found = found3[0:32] + found3[32:64] + found3[64:96]
    kinds = head[3:4, :]
    bed_row = head[1:2, :]
    is_remote = (kinds == 1.0) | (kinds == 2.0)
    spot = jnp.where(kinds == 1.0, found[8:9], jnp.where(kinds == 2.0, found[16:17], found[0:1]))
    bed_far = jnp.where(kinds == 1.0, found[9:10], jnp.where(kinds == 2.0, found[17:18], found[1:2]))
    table[T_LOCAL:T_LOCAL + 1] = jnp.where(kinds == 0.0, spot, -1.0)
    table[T_REMOTE:T_REMOTE + 1] = jnp.where(is_remote, spot, -1.0)
    table[BED:BED + 1] = bed_row
    table[BED_DOWN:BED_DOWN + 1] = jnp.where(kinds == 3.0, bed_row - 1.0, bed_far)
    table[9:16] = jnp.zeros((7, count), F32)

    split_table = pieces(table[...])
    rows3 = dot_nt(split_table, perm[...])
    table[...] = rows3[0:16] + rows3[16:32] + rows3[32:48]
    for hop in range(2):
        @pl.when(has_lower(hop))
        def _(hop=hop):
            dn(M_TABLE, hop, table.at[pl.ds(0, 8), pl.ds(hop * SLOTS, SLOTS)], table_in.at[hop]).start()

    lanes = lax.broadcasted_iota(jnp.int32, (128, count), 1).astype(F32)

    def spread(columns, base, size, target_column, last):
        for k in range(BED, last):
            par[k - BED, base:base + size] = jnp.broadcast_to(columns[:, k:k + 1], (size, members))
        for t in range(size // 128):
            emap[base + t * 128:base + (t + 1) * 128] = jnp.where(
                columns[t * 128:(t + 1) * 128, target_column:target_column + 1] == lanes, 1.0, 0.0
            ).astype(BF16)

    for c in range(count // SLOTS):
        cols3 = dot_nt(perm[chunk(c)], split_table)
        spread(cols3[:, 0:16] + cols3[:, 16:32] + cols3[:, 32:48], c * SLOTS, SLOTS, T_LOCAL, 9)
    one_hot_rows(smap, table[T_LOCAL:T_LOCAL + 1], 0, count)

    eye = (
        lax.broadcasted_iota(jnp.int32, (SLOTS, SLOTS), 0) == lax.broadcasted_iota(jnp.int32, (SLOTS, SLOTS), 1)
    ).astype(BF16)
    blank = jnp.zeros((8, SLOTS), F32)
    for hop in range(2):
        @pl.when(has_upper(hop))
        def _(hop=hop):
            dn(M_TABLE, hop, table.at[pl.ds(0, 8), pl.ds(hop * SLOTS, SLOTS)], table_in.at[hop]).wait_recv()
        cols3 = dot_nt(eye, pieces(jnp.concatenate([table_in[hop], blank], axis=0)))
        spread(cols3[:, 0:16] + cols3[:, 16:32] + cols3[:, 32:48], count + hop * SLOTS, SLOTS, T_REMOTE, 8)

    def send_up(step):
        for hop in range(2):
            up_out[step, hop] = joined(emap[count + hop * SLOTS:count + (hop + 1) * SLOTS], split_a[...])

            @pl.when(has_upper(hop))
            def _(hop=hop):
                up(M_UP + 2 * step, hop, up_out.at[step, hop], up_in.at[step, hop]).start()

    split_into(split_a, h_buf.at[0])
    send_up(0)
    for hop in range(2):
        one_hot_rows(smap, table_in[hop, T_REMOTE:T_REMOTE + 1], count + hop * SLOTS, SLOTS)
    for c in range(count // SLOTS):
        r_buf[chunk(c)] = joined(perm[chunk(c)], split_c[...]) * TIME_STEP

    eye8 = eye[:128, :128]
    place_t = dot_nt(eye8, pieces(jnp.concatenate([place, jnp.zeros((16 - tiles, 128), F32)], axis=0)))
    place_t = place_t[:, 0:16] + place_t[:, 16:32] + place_t[:, 32:48]
    for t in range(tiles):
        unperm[t * 128:(t + 1) * 128] = jnp.where(place_t[:, t:t + 1] == lanes, 1.0, 0.0).astype(BF16)

    def momentum(rows, q, h, hd):
        bed = par[0, rows, :]
        bed_down = par[1, rows, :]
        level = bed + h
        level_down = bed_down + hd
        deep = jnp.maximum(jnp.maximum(level, level_down) - jnp.maximum(bed, bed_down), DEPTH_FLOOR)
        root = jnp.exp2(jnp.log2(deep) * (-7.0 / 3.0))
        moved = (q - deep * (level_down - level) * par[2, rows, :]) / (
            1.0 + par[5, rows, :] * jnp.abs(q) * root
        )
        q = jnp.minimum(moved, h * par[3, rows, :])
        q_buf[rows, :] = q
        high, low = halves(q * par[4, rows, :])
        edge_split[rows, :members] = high
        edge_split[rows, members:] = low

    block = 64
    for step in range(STEPS):
        last = step == STEPS - 1
        for c in range(count // SLOTS):
            hd_buf[chunk(c)] = joined(emap[chunk(c)], split_a[...])

        def inner(t, carry):
            rows = pl.ds(pl.multiple_of(2 * SLOTS + t * block, block), block)
            momentum(rows, q_buf[rows, :], h_buf[step, rows, :], hd_buf[rows, :])
            return carry
        if step == 0:
            for hop in range(2):
                @pl.when(has_lower(hop))
                def _(hop=hop):
                    dn(M_FLOW, hop, q_buf.at[pl.ds(hop * SLOTS, SLOTS)], q_buf.at[pl.ds(count + hop * SLOTS, SLOTS)]).wait_send()
        lax.fori_loop(0, (count - 2 * SLOTS) // block, inner, 0)
        for c in range(count // SLOTS):
            acc[chunk(c)] = joined(smap[chunk(c), 2 * SLOTS:count], edge_split[2 * SLOTS:count])
        for hop in range(2):
            @pl.when(has_lower(hop))
            def _(hop=hop):
                up(M_UP + 2 * step, hop, up_out.at[step, hop], up_in.at[step, hop]).wait_recv()

            def outer(t, carry):
                at = pl.ds(pl.multiple_of(t * block, block), block)
                rows = pl.ds(pl.multiple_of(hop * SLOTS + t * block, block), block)
                momentum(rows, q_buf[rows, :], h_buf[step, rows, :], hd_buf[rows, :] + up_in[step, hop, at, :])
                return carry
            lax.fori_loop(0, SLOTS // block, outer, 0)

        if last:
            for t in range(count // 128):
                rows = slice(t * 128, (t + 1) * 128)
                high, low = halves(q_buf[rows])
                split_b[rows, :members] = high
                split_b[rows, members:] = low
            for c in range(count // SLOTS):
                new_flow[chunk(c)] = joined(unperm[chunk(c)], split_b[...])
            one = jnp.ones((16, members), BF16)
            high, low = halves(new_flow[...])
            sums[...] = (dot_nt(one, high) + dot_nt(one, low))[0:8]
            for d in range(1, n_ens):
                pltpu.make_async_remote_copy(
                    src_ref=sums, dst_ref=sums_in.at[d - 1], send_sem=send_sem.at[M_SUM + d - 1],
                    recv_sem=recv_sem.at[M_SUM + d - 1],
                    device_id={"ens": lax.rem(e + d, n_ens)}, device_id_type=MESH,
                ).start()

        for hop in range(2):
            @pl.when(has_upper(hop))
            def _(hop=hop):
                if step == 0:
                    dn(M_FLOW, hop, q_buf.at[pl.ds(hop * SLOTS, SLOTS)], q_buf.at[pl.ds(count + hop * SLOTS, SLOTS)]).wait_recv()
                dn(M_DOWN + 2 * step, hop, h_buf.at[step, pl.ds(hop * SLOTS, SLOTS)], down_in.at[step, hop]).wait_recv()

            def ghost(t, carry):
                at = pl.ds(pl.multiple_of(t * block, block), block)
                rows = pl.ds(pl.multiple_of(count + hop * SLOTS + t * block, block), block)
                momentum(rows, q_buf[rows, :], down_in[step, hop, at, :], up_out[step, hop, at, :])
                return carry
            lax.fori_loop(0, SLOTS // block, ghost, 0)

        for c in range(count // SLOTS):
            arriving = (
                acc[chunk(c)]
                + joined(smap[chunk(c), 0:2 * SLOTS], edge_split[0:2 * SLOTS])
                + joined(smap[chunk(c), count:], edge_split[count:])
            )
            fresh = h_buf[step, chunk(c)] + (
                r_buf[chunk(c)] + (arriving - q_buf[chunk(c)] * par[4, chunk(c)]) * par[6, chunk(c)]
            )
            h_buf[step + 1, chunk(c)] = fresh
            if c < 2 and not last:
                @pl.when(has_lower(c))
                def _(c=c):
                    dn(M_DOWN + 2 * step + 2, c, h_buf.at[step + 1, pl.ds(c * SLOTS, SLOTS)], down_in.at[step + 1, c]).start()
            high, low = halves(fresh)
            split_a[chunk(c), :members] = high
            split_a[chunk(c), members:] = low
        if not last:
            send_up(step + 1)

    for c in range(count // SLOTS):
        new_depth[chunk(c)] = joined(unperm[chunk(c)], split_a[...])

    total = sums[...]
    for d in range(1, n_ens):
        copy = pltpu.make_async_remote_copy(
            src_ref=sums, dst_ref=sums_in.at[d - 1], send_sem=send_sem.at[M_SUM + d - 1],
            recv_sem=recv_sem.at[M_SUM + d - 1],
            device_id={"ens": lax.rem(e + d, n_ens)}, device_id_type=MESH,
        )
        copy.wait()
        total = total + sums_in[d - 1]
    mean_out[...] = total * (1.0 / (n_ens * members))

    for hop in range(2):
        @pl.when(has_lower(hop))
        def _(hop=hop):
            dn(M_TABLE, hop, table.at[pl.ds(0, 8), pl.ds(hop * SLOTS, SLOTS)], table_in.at[hop]).wait_send()
            for step in range(STEPS):
                dn(M_DOWN + 2 * step, hop, h_buf.at[step, pl.ds(hop * SLOTS, SLOTS)], down_in.at[step, hop]).wait_send()

        @pl.when(has_upper(hop))
        def _(hop=hop):
            up(M_HEAD, hop, head, head_in.at[hop]).wait_send()
            for step in range(STEPS):
                up(M_UP + 2 * step, hop, up_out.at[step, hop], up_in.at[step, hop]).wait_send()


def per_device(downstream, bed_level, reach_length, channel_width, roughness, depth, flow, runoff):
    n_basin = lax.axis_size("basin")
    n_ens = lax.axis_size("ens")
    count, members = depth.shape
    edges = count + 2 * SLOTS
    messages = M_SUM + n_ens - 1
    tile = lambda x: x.reshape(count // 128, 128)
    whole = pl.BlockSpec(memory_space=pltpu.VMEM)
    new_depth, new_flow, mean = pl.pallas_call(
        functools.partial(kernel, n_basin, n_ens),
        out_shape=(
            jax.ShapeDtypeStruct((count, members), F32),
            jax.ShapeDtypeStruct((count, members), F32),
            jax.ShapeDtypeStruct((8, count), F32),
        ),
        in_specs=[whole] * 8,
        out_specs=(whole,) * 3,
        scratch_shapes=[
            pltpu.VMEM((8, count), F32),
            pltpu.VMEM((2, 8, count), F32),
            pltpu.VMEM((16, count), F32),
            pltpu.VMEM((2, 8, SLOTS), F32),
            pltpu.VMEM((count, count), BF16),
            pltpu.VMEM((count, count), BF16),
            pltpu.VMEM((count, count), BF16),
            pltpu.VMEM((edges, count), BF16),
            pltpu.VMEM((count, edges), BF16),
            pltpu.VMEM((7, edges, members), F32),
            pltpu.VMEM((STEPS + 1, count, members), F32),
            pltpu.VMEM((edges, members), F32),
            pltpu.VMEM((count, members), F32),
            pltpu.VMEM((count, 2 * members), BF16),
            pltpu.VMEM((count, 2 * members), BF16),
            pltpu.VMEM((count, 2 * members), BF16),
            pltpu.VMEM((count, members), F32),
            pltpu.VMEM((STEPS, 2, SLOTS, members), F32),
            pltpu.VMEM((STEPS, 2, SLOTS, members), F32),
            pltpu.VMEM((STEPS, 2, SLOTS, members), F32),
            pltpu.VMEM((count, members), F32),
            pltpu.VMEM((edges, 2 * members), BF16),
            pltpu.VMEM((8, count), F32),
            pltpu.VMEM((n_ens - 1, 8, count), F32),
            pltpu.SemaphoreType.DMA((messages,)),
            pltpu.SemaphoreType.DMA((messages,)),
        ],
        compiler_params=pltpu.CompilerParams(
            collective_id=0, has_side_effects=True, vmem_limit_bytes=56 * 1024 * 1024
        ),
    )(tile(downstream), tile(bed_level), tile(reach_length), tile(channel_width), tile(roughness), depth, flow, runoff)
    return new_depth, new_flow, mean[0]


def solution(mesh):
    cells, both = P("basin"), P("basin", "ens")
    return jax.shard_map(
        per_device,
        mesh=mesh,
        in_specs=(cells,) * 5 + (both,) * 3,
        out_specs=(both, both, cells),
        check_vma=False,
    )
```

```python
import functools

import jax
import jax.numpy as jnp
from jax import lax
from jax.experimental import pallas as pl
from jax.experimental.pallas import tpu as pltpu
from jax.sharding import PartitionSpec as P

SLOTS = 256
STEPS = 4
GRAVITY = 9.81
TIME_STEP = 30.0
DEPTH_FLOOR = 0.25

BF16 = jnp.bfloat16
F32 = jnp.float32
MESH = pl.DeviceIdType.MESH

T_LOCAL, T_REMOTE, BED, BED_DOWN, SLOPE_K, CAP, WIDTH, FRICTION, INV_AREA = range(9)
M_HEAD, M_TABLE, M_FLOW, M_DOWN, M_UP = 0, 2, 4, 6, 6 + 2 * STEPS
M_SUM = 6 + 4 * STEPS


def dot(a, b):
    return jnp.dot(a, b, preferred_element_type=F32)


def dot_nt(a, b):
    return lax.dot_general(a, b, (((1,), (1,)), ((), ())), preferred_element_type=F32)


def pieces(x):
    high = x.astype(BF16)
    rest = x - high.astype(F32)
    middle = rest.astype(BF16)
    low = (rest - middle.astype(F32)).astype(BF16)
    return jnp.concatenate([high, middle, low], axis=0)


def halves(x):
    high = x.astype(BF16)
    return high, (x - high.astype(F32)).astype(BF16)


def kernel(
    n_basin, n_ens, ds_ref, bed_ref, len_ref, wid_ref, rough_ref, depth_ref, flow_ref, runoff_ref,
    new_depth, new_flow, mean_out, place_out,
    head, head_in, table, table_in, perm, tmap, emap, smap, par, h_buf, q_buf, r_buf,
    split_a, split_b, split_c, hd_buf, up_out, up_in, down_in, acc, edge_split, sums, sums_in,
    send_sem, recv_sem,
):
    count = depth_ref.shape[0]
    members = depth_ref.shape[1]
    tiles = count // 128
    p = lax.axis_index("basin")
    e = lax.axis_index("ens")

    def dn(index, hop, src, dst):
        return pltpu.make_async_remote_copy(
            src_ref=src, dst_ref=dst, send_sem=send_sem.at[index + hop],
            recv_sem=recv_sem.at[index + hop],
            device_id={"basin": lax.rem(p + hop + 1, n_basin)}, device_id_type=MESH,
        )

    def up(index, hop, src, dst):
        return pltpu.make_async_remote_copy(
            src_ref=src, dst_ref=dst, send_sem=send_sem.at[index + hop],
            recv_sem=recv_sem.at[index + hop],
            device_id={"basin": lax.rem(p + n_basin - hop - 1, n_basin)}, device_id_type=MESH,
        )

    def has_lower(hop):
        return p + (hop + 1) < n_basin

    def has_upper(hop):
        return p >= hop + 1

    barrier = pltpu.get_barrier_semaphore()
    for hop in range(2):
        @pl.when(has_lower(hop))
        def _(hop=hop):
            pl.semaphore_signal(barrier, inc=1, device_id={"basin": p + hop + 1}, device_id_type=MESH)

        @pl.when(has_upper(hop))
        def _(hop=hop):
            pl.semaphore_signal(barrier, inc=1, device_id={"basin": p - hop - 1}, device_id_type=MESH)
    for d in range(1, n_ens):
        pl.semaphore_signal(barrier, inc=1, device_id={"ens": lax.rem(e + d, n_ens)}, device_id_type=MESH)

    rel = ds_ref[...] - p * count
    own = lax.broadcasted_iota(jnp.int32, (tiles, 128), 0) * 128 + lax.broadcasted_iota(
        jnp.int32, (tiles, 128), 1
    )
    near = (rel >= count) & (rel < 2 * count)
    far = rel >= 2 * count
    mouth = rel == own
    target = rel - jnp.where(near, count, 0) - jnp.where(far, 2 * count, 0)
    kind = jnp.where(near, 1.0, jnp.where(far, 2.0, jnp.where(mouth, 3.0, 0.0)))
    before = (
        lax.broadcasted_iota(jnp.int32, (128, 128), 0) < lax.broadcasted_iota(jnp.int32, (128, 128), 1)
    ).astype(BF16)
    ones = jnp.ones((128, 128), BF16)

    def ranks(mask):
        m = mask.astype(F32).astype(BF16)
        within = dot(m, before)
        totals = dot(m, ones)
        offsets, total = [], jnp.zeros((1, 128), F32)
        for t in range(tiles):
            offsets.append(total)
            total = total + totals[t:t + 1]
        return within + jnp.concatenate(offsets, axis=0), total

    rank1, n1 = ranks(near)
    rank2, n2 = ranks(far)
    rank0, _ = ranks(jnp.logical_not(near | far))
    gap1 = SLOTS - n1
    gap2 = SLOTS - n2
    place0 = jnp.where(
        rank0 < gap1, n1 + rank0,
        jnp.where(rank0 < gap1 + gap2, SLOTS + n2 + (rank0 - gap1), n1 + n2 + rank0),
    )
    place = jnp.where(near, rank1, jnp.where(far, SLOTS + rank2, place0))

    def to_row(ref, row, value):
        for t in range(tiles):
            ref[row:row + 1, t * 128:(t + 1) * 128] = value[t:t + 1]

    length = len_ref[...]
    width = wid_ref[...]
    rough = rough_ref[...]
    to_row(head, 0, place)
    to_row(head, 1, bed_ref[...])
    to_row(head, 2, target.astype(F32))
    to_row(head, 3, kind)
    head[4:8] = jnp.zeros((4, count), F32)
    to_row(table, SLOPE_K, (GRAVITY * TIME_STEP) / length)
    to_row(table, CAP, length / (2.0 * TIME_STEP))
    to_row(table, WIDTH, width)
    to_row(table, FRICTION, GRAVITY * TIME_STEP * rough * rough)
    to_row(table, INV_AREA, TIME_STEP / (width * length))

    peers = n_ens - 1
    for hop in range(2):
        peers = peers + lax.div(p + (n_basin - hop - 1), n_basin)
        peers = peers + lax.div(2 * n_basin - p - hop - 2, n_basin)
    pl.semaphore_wait(barrier, peers)

    for hop in range(2):
        @pl.when(has_upper(hop))
        def _(hop=hop):
            up(M_HEAD, hop, head, head_in.at[hop]).start()

    for hop in range(2):
        @pl.when(jnp.logical_not(has_upper(hop)))
        def _(hop=hop):
            rows = lax.broadcasted_iota(jnp.int32, (8, SLOTS), 0)
            table_in[hop] = jnp.where(rows == T_REMOTE, -1.0, 1.0)
            q_buf[count + hop * SLOTS:count + (hop + 1) * SLOTS] = jnp.zeros((SLOTS, members), F32)
            for step in range(STEPS):
                down_in[step, hop] = jnp.zeros((SLOTS, members), F32)

        @pl.when(jnp.logical_not(has_lower(hop)))
        def _(hop=hop):
            head_in[hop] = jnp.zeros((8, count), F32)
            for step in range(STEPS):
                up_in[step, hop] = jnp.zeros((SLOTS, members), F32)

    def one_hot_rows(ref, index_row, base, columns):
        def body(t, carry):
            rows = pl.ds(pl.multiple_of(t * 64, 64), 64)
            at = (lax.broadcasted_iota(jnp.int32, (64, columns), 0) + t * 64).astype(F32)
            ref[rows, base:base + columns] = jnp.where(at == index_row, 1.0, 0.0).astype(BF16)
            return carry
        lax.fori_loop(0, count // 64, body, 0)

    one_hot_rows(perm, head[0:1, :], 0, count)

    def split_into(dst, src):
        def body(t, carry):
            rows = pl.ds(pl.multiple_of(t * 128, 128), 128)
            high, low = halves(src[rows, :])
            dst[rows, :members] = high
            dst[rows, members:] = low
            return carry
        lax.fori_loop(0, count // 128, body, 0)

    split_into(split_a, depth_ref)
    split_into(split_b, flow_ref)
    split_into(split_c, runoff_ref)

    def joined(a, b):
        out = dot(a, b)
        return out[:, :members] + out[:, members:]

    def chunk(c, size=SLOTS):
        return slice(c * size, (c + 1) * size)

    for c in range(count // SLOTS):
        h_buf[0, chunk(c)] = joined(perm[chunk(c)], split_a[...])
        q_buf[chunk(c)] = joined(perm[chunk(c)], split_b[...])

    one_hot_rows(tmap, head[2:3, :], 0, count)
    for hop in range(2):
        @pl.when(has_lower(hop))
        def _(hop=hop):
            up(M_HEAD, hop, head, head_in.at[hop]).wait_recv()
    looked = jnp.concatenate([head[...], head_in[0], head_in[1], jnp.zeros((8, count), F32)], axis=0)
    found3 = dot(pieces(looked), tmap[...])
    found = found3[0:32] + found3[32:64] + found3[64:96]
    kinds = head[3:4, :]
    bed_row = head[1:2, :]
    is_remote = (kinds == 1.0) | (kinds == 2.0)
    spot = jnp.where(kinds == 1.0, found[8:9], jnp.where(kinds == 2.0, found[16:17], found[0:1]))
    bed_far = jnp.where(kinds == 1.0, found[9:10], jnp.where(kinds == 2.0, found[17:18], found[1:2]))
    table[T_LOCAL:T_LOCAL + 1] = jnp.where(kinds == 0.0, spot, -1.0)
    table[T_REMOTE:T_REMOTE + 1] = jnp.where(is_remote, spot, -1.0)
    table[BED:BED + 1] = bed_row
    table[BED_DOWN:BED_DOWN + 1] = jnp.where(kinds == 3.0, bed_row - 1.0, bed_far)
    table[9:16] = jnp.zeros((7, count), F32)

    split_table = pieces(table[...])
    rows3 = dot_nt(split_table, perm[...])
    table[...] = rows3[0:16] + rows3[16:32] + rows3[32:48]
    for hop in range(2):
        @pl.when(has_lower(hop))
        def _(hop=hop):
            dn(M_TABLE, hop, table.at[pl.ds(0, 8), pl.ds(hop * SLOTS, SLOTS)], table_in.at[hop]).start()
    for hop in range(2):
        @pl.when(has_lower(hop))
        def _(hop=hop):
            dn(M_DOWN, hop, h_buf.at[0, pl.ds(hop * SLOTS, SLOTS)], down_in.at[0, hop]).start()
            dn(M_FLOW, hop, q_buf.at[pl.ds(hop * SLOTS, SLOTS)], q_buf.at[pl.ds(count + hop * SLOTS, SLOTS)]).start()

    lanes = lax.broadcasted_iota(jnp.int32, (128, count), 1).astype(F32)

    def spread(columns, base, size, target_column, last):
        for k in range(BED, last):
            par[k - BED, base:base + size] = jnp.broadcast_to(columns[:, k:k + 1], (size, members))
        for t in range(size // 128):
            emap[base + t * 128:base + (t + 1) * 128] = jnp.where(
                columns[t * 128:(t + 1) * 128, target_column:target_column + 1] == lanes, 1.0, 0.0
            ).astype(BF16)

    for c in range(count // SLOTS):
        cols3 = dot_nt(perm[chunk(c)], split_table)
        spread(cols3[:, 0:16] + cols3[:, 16:32] + cols3[:, 32:48], c * SLOTS, SLOTS, T_LOCAL, 9)
    one_hot_rows(smap, table[T_LOCAL:T_LOCAL + 1], 0, count)

    eye = (
        lax.broadcasted_iota(jnp.int32, (SLOTS, SLOTS), 0) == lax.broadcasted_iota(jnp.int32, (SLOTS, SLOTS), 1)
    ).astype(BF16)
    blank = jnp.zeros((8, SLOTS), F32)
    for hop in range(2):
        @pl.when(has_upper(hop))
        def _(hop=hop):
            dn(M_TABLE, hop, table.at[pl.ds(0, 8), pl.ds(hop * SLOTS, SLOTS)], table_in.at[hop]).wait_recv()
        cols3 = dot_nt(eye, pieces(jnp.concatenate([table_in[hop], blank], axis=0)))
        spread(cols3[:, 0:16] + cols3[:, 16:32] + cols3[:, 32:48], count + hop * SLOTS, SLOTS, T_REMOTE, 8)

    def send_up(step):
        for hop in range(2):
            up_out[step, hop] = joined(emap[count + hop * SLOTS:count + (hop + 1) * SLOTS], split_a[...])

            @pl.when(has_upper(hop))
            def _(hop=hop):
                up(M_UP + 2 * step, hop, up_out.at[step, hop], up_in.at[step, hop]).start()

    split_into(split_a, h_buf.at[0])
    send_up(0)
    for hop in range(2):
        one_hot_rows(smap, table_in[hop, T_REMOTE:T_REMOTE + 1], count + hop * SLOTS, SLOTS)
    for c in range(count // SLOTS):
        r_buf[chunk(c)] = joined(perm[chunk(c)], split_c[...]) * TIME_STEP

    def momentum(rows, q, h, hd):
        bed = par[0, rows, :]
        bed_down = par[1, rows, :]
        level = bed + h
        level_down = bed_down + hd
        deep = jnp.maximum(jnp.maximum(level, level_down) - jnp.maximum(bed, bed_down), DEPTH_FLOOR)
        root = jnp.exp2(jnp.log2(deep) * (-7.0 / 3.0))
        moved = (q - deep * (level_down - level) * par[2, rows, :]) / (
            1.0 + par[5, rows, :] * jnp.abs(q) * root
        )
        q = jnp.minimum(moved, h * par[3, rows, :])
        q_buf[rows, :] = q
        high, low = halves(q * par[4, rows, :])
        edge_split[rows, :members] = high
        edge_split[rows, members:] = low

    block = 128
    for step in range(STEPS):
        last = step == STEPS - 1
        for c in range(count // SLOTS):
            hd_buf[chunk(c)] = joined(emap[chunk(c)], split_a[...])

        def inner(t, carry):
            rows = pl.ds(pl.multiple_of(2 * SLOTS + t * block, block), block)
            momentum(rows, q_buf[rows, :], h_buf[step, rows, :], hd_buf[rows, :])
            return carry
        if step == 0:
            for hop in range(2):
                @pl.when(has_lower(hop))
                def _(hop=hop):
                    dn(M_FLOW, hop, q_buf.at[pl.ds(hop * SLOTS, SLOTS)], q_buf.at[pl.ds(count + hop * SLOTS, SLOTS)]).wait_send()
        lax.fori_loop(0, (count - 2 * SLOTS) // block, inner, 0)
        for c in range(count // SLOTS):
            acc[chunk(c)] = joined(smap[chunk(c), 2 * SLOTS:count], edge_split[2 * SLOTS:count])
        for hop in range(2):
            @pl.when(has_lower(hop))
            def _(hop=hop):
                up(M_UP + 2 * step, hop, up_out.at[step, hop], up_in.at[step, hop]).wait_recv()

            def outer(t, carry):
                at = pl.ds(pl.multiple_of(t * block, block), block)
                rows = pl.ds(pl.multiple_of(hop * SLOTS + t * block, block), block)
                momentum(rows, q_buf[rows, :], h_buf[step, rows, :], hd_buf[rows, :] + up_in[step, hop, at, :])
                return carry
            lax.fori_loop(0, SLOTS // block, outer, 0)

        if last:
            one = jnp.ones((16, members), BF16)
            for c in range(count // SLOTS):
                now = q_buf[chunk(c)]
                new_flow[chunk(c)] = now
                high, low = halves(now)
                sums[:, chunk(c)] = (dot_nt(one, high) + dot_nt(one, low))[0:8]
            for d in range(1, n_ens):
                pltpu.make_async_remote_copy(
                    src_ref=sums, dst_ref=sums_in.at[d - 1], send_sem=send_sem.at[M_SUM + d - 1],
                    recv_sem=recv_sem.at[M_SUM + d - 1],
                    device_id={"ens": lax.rem(e + d, n_ens)}, device_id_type=MESH,
                ).start()

        for hop in range(2):
            @pl.when(has_upper(hop))
            def _(hop=hop):
                if step == 0:
                    dn(M_FLOW, hop, q_buf.at[pl.ds(hop * SLOTS, SLOTS)], q_buf.at[pl.ds(count + hop * SLOTS, SLOTS)]).wait_recv()
                dn(M_DOWN + 2 * step, hop, h_buf.at[step, pl.ds(hop * SLOTS, SLOTS)], down_in.at[step, hop]).wait_recv()

            def ghost(t, carry):
                at = pl.ds(pl.multiple_of(t * block, block), block)
                rows = pl.ds(pl.multiple_of(count + hop * SLOTS + t * block, block), block)
                momentum(rows, q_buf[rows, :], down_in[step, hop, at, :], up_out[step, hop, at, :])
                return carry
            lax.fori_loop(0, SLOTS // block, ghost, 0)

        for c in range(count // SLOTS):
            arriving = (
                acc[chunk(c)]
                + joined(smap[chunk(c), 0:2 * SLOTS], edge_split[0:2 * SLOTS])
                + joined(smap[chunk(c), count:], edge_split[count:])
            )
            fresh = h_buf[step, chunk(c)] + (
                r_buf[chunk(c)] + (arriving - q_buf[chunk(c)] * par[4, chunk(c)]) * par[6, chunk(c)]
            )
            if last:
                new_depth[chunk(c)] = fresh
                continue
            h_buf[step + 1, chunk(c)] = fresh
            if c < 2:
                @pl.when(has_lower(c))
                def _(c=c):
                    dn(M_DOWN + 2 * step + 2, c, h_buf.at[step + 1, pl.ds(c * SLOTS, SLOTS)], down_in.at[step + 1, c]).start()
            high, low = halves(fresh)
            split_a[chunk(c), :members] = high
            split_a[chunk(c), members:] = low
        if not last:
            send_up(step + 1)

    total = sums[...]
    for d in range(1, n_ens):
        copy = pltpu.make_async_remote_copy(
            src_ref=sums, dst_ref=sums_in.at[d - 1], send_sem=send_sem.at[M_SUM + d - 1],
            recv_sem=recv_sem.at[M_SUM + d - 1],
            device_id={"ens": lax.rem(e + d, n_ens)}, device_id_type=MESH,
        )
        copy.wait()
        total = total + sums_in[d - 1]
    mean_out[...] = total * (1.0 / (n_ens * members))
    place_out[...] = place

    for hop in range(2):
        @pl.when(has_lower(hop))
        def _(hop=hop):
            dn(M_TABLE, hop, table.at[pl.ds(0, 8), pl.ds(hop * SLOTS, SLOTS)], table_in.at[hop]).wait_send()
            for step in range(STEPS):
                dn(M_DOWN + 2 * step, hop, h_buf.at[step, pl.ds(hop * SLOTS, SLOTS)], down_in.at[step, hop]).wait_send()

        @pl.when(has_upper(hop))
        def _(hop=hop):
            up(M_HEAD, hop, head, head_in.at[hop]).wait_send()
            for step in range(STEPS):
                up(M_UP + 2 * step, hop, up_out.at[step, hop], up_in.at[step, hop]).wait_send()


def own_order(depth_ref, flow_ref, mean_ref, place_ref, new_depth, new_flow, mean_out, split):
    count, members = depth_ref.shape
    tiles = count // 128
    for t in range(tiles):
        rows = slice(t * 128, (t + 1) * 128)
        for k, ref in enumerate((depth_ref, flow_ref)):
            high, low = halves(ref[rows])
            split[rows, 2 * k * members:(2 * k + 1) * members] = high
            split[rows, (2 * k + 1) * members:(2 * k + 2) * members] = low
    eye = (
        lax.broadcasted_iota(jnp.int32, (128, 128), 0) == lax.broadcasted_iota(jnp.int32, (128, 128), 1)
    ).astype(BF16)
    place = jnp.concatenate([place_ref[...], jnp.zeros((16 - tiles, 128), F32)], axis=0)
    place_t = dot_nt(eye, pieces(place))
    place_t = place_t[:, 0:16] + place_t[:, 16:32] + place_t[:, 32:48]
    lanes = lax.broadcasted_iota(jnp.int32, (128, count), 1).astype(F32)
    mean = pieces(jnp.concatenate([mean_ref[...], mean_ref[...]], axis=0))
    for t in range(tiles):
        rows = slice(t * 128, (t + 1) * 128)
        back = jnp.where(place_t[:, t:t + 1] == lanes, 1.0, 0.0).astype(BF16)
        out = dot(back, split[...])
        new_depth[rows] = out[:, :members] + out[:, members:2 * members]
        new_flow[rows] = out[:, 2 * members:3 * members] + out[:, 3 * members:]
        row = dot_nt(mean, back)
        mean_out[t:t + 1] = row[0:1] + row[16:17] + row[32:33]


def per_device(downstream, bed_level, reach_length, channel_width, roughness, depth, flow, runoff):
    n_basin = lax.axis_size("basin")
    n_ens = lax.axis_size("ens")
    count, members = depth.shape
    edges = count + 2 * SLOTS
    messages = M_SUM + n_ens - 1
    tile = lambda x: x.reshape(count // 128, 128)
    whole = pl.BlockSpec(memory_space=pltpu.VMEM)
    moved = pl.pallas_call(
        functools.partial(kernel, n_basin, n_ens),
        out_shape=(
            jax.ShapeDtypeStruct((count, members), F32),
            jax.ShapeDtypeStruct((count, members), F32),
            jax.ShapeDtypeStruct((8, count), F32),
            jax.ShapeDtypeStruct((count // 128, 128), F32),
        ),
        in_specs=[whole] * 8,
        out_specs=(whole,) * 4,
        scratch_shapes=[
            pltpu.VMEM((8, count), F32),
            pltpu.VMEM((2, 8, count), F32),
            pltpu.VMEM((16, count), F32),
            pltpu.VMEM((2, 8, SLOTS), F32),
            pltpu.VMEM((count, count), BF16),
            pltpu.VMEM((count, count), BF16),
            pltpu.VMEM((edges, count), BF16),
            pltpu.VMEM((count, edges), BF16),
            pltpu.VMEM((7, edges, members), F32),
            pltpu.VMEM((STEPS, count, members), F32),
            pltpu.VMEM((edges, members), F32),
            pltpu.VMEM((count, members), F32),
            pltpu.VMEM((count, 2 * members), BF16),
            pltpu.VMEM((count, 2 * members), BF16),
            pltpu.VMEM((count, 2 * members), BF16),
            pltpu.VMEM((count, members), F32),
            pltpu.VMEM((STEPS, 2, SLOTS, members), F32),
            pltpu.VMEM((STEPS, 2, SLOTS, members), F32),
            pltpu.VMEM((STEPS, 2, SLOTS, members), F32),
            pltpu.VMEM((count, members), F32),
            pltpu.VMEM((edges, 2 * members), BF16),
            pltpu.VMEM((8, count), F32),
            pltpu.VMEM((n_ens - 1, 8, count), F32),
            pltpu.SemaphoreType.DMA((messages,)),
            pltpu.SemaphoreType.DMA((messages,)),
        ],
        compiler_params=pltpu.CompilerParams(
            collective_id=0, has_side_effects=True, vmem_limit_bytes=56 * 1024 * 1024
        ),
    )(tile(downstream), tile(bed_level), tile(reach_length), tile(channel_width), tile(roughness), depth, flow, runoff)
    new_depth, new_flow, mean = pl.pallas_call(
        own_order,
        out_shape=(
            jax.ShapeDtypeStruct((count, members), F32),
            jax.ShapeDtypeStruct((count, members), F32),
            jax.ShapeDtypeStruct((count // 128, 128), F32),
        ),
        in_specs=[whole] * 4,
        out_specs=(whole,) * 3,
        scratch_shapes=[pltpu.VMEM((count, 4 * members), BF16)],
        compiler_params=pltpu.CompilerParams(vmem_limit_bytes=56 * 1024 * 1024),
    )(*moved)
    return new_depth, new_flow, mean.reshape(count)


def solution(mesh):
    cells, both = P("basin"), P("basin", "ens")
    return jax.shard_map(
        per_device,
        mesh=mesh,
        in_specs=(cells,) * 5 + (both,) * 3,
        out_specs=(both, both, cells),
        check_vma=False,
    )
```
